256 devices in a mesh: row: 8 (over z_lo, x), col: 32 (over z_hi, y, core).
Axes of the slice: x: 4, y: 4, z: 8 (z_hi: 4, z_lo: 2; z = z_hi * 2 + z_lo), core: 2. Of those that a mesh axis runs over, the one named last changes fastest.
Arguments:
- activations: bfloat16 [262144, 896], P(('row', 'col')), may hold values from -6 to 6
- cotangent: bfloat16 [262144, 896], P(('row', 'col')), may hold values from -6 to 6
- inner_first: bfloat16 [28672, 7168], P('col', 'row'), may hold values from -6 to 6
- inner_second: bfloat16 [7168, 28672], P('row', 'col'), may hold values from -6 to 6
- outer_first: float32 [896, 7168], P('col', 'row'), may hold values from -6 to 6
- momentum_first: float32 [896, 7168], P('col', 'row'), may hold values from -3 to 3
- outer_second: float32 [896, 28672], P('row', 'col'), may hold values from -6 to 6
- momentum_second: float32 [896, 28672], P('row', 'col'), may hold values from -3 to 3
Outputs:
- new_outer_first: float32 [896, 7168], P('col', 'row')
- new_momentum_first: float32 [896, 7168], P('col', 'row')
- new_outer_second: float32 [896, 28672], P('row', 'col')
- new_momentum_second: float32 [896, 28672], P('row', 'col')
- reset_first: bfloat16 [28672, 7168], P('col', 'row')
- reset_second: bfloat16 [7168, 28672], P('row', 'col')
The draws below stay inside these ranges and needn't reach their ends.
All inputs are finite; a program needn't handle non-finite values.
Results may differ from the reference program's by a relative error of at most 0.003.
Values may be sent and summed in bfloat16 or wider, within the bound.
No kernel may reach another device: no remote copies, remote signals or barrier semaphores. Data moves between devices by JAX's collectives and lax.ppermute only.
A program may use at most 64 MiB of HBM per device.

```python
import jax
import jax.numpy as jnp
from jax import lax

D = 896
TOK_DEV = 1024
TOKENS = 262144
N_ROW = 8
N_COL = 32


def block_levels(rng, dims, pieces, smallest, top_value):
    def one(position, shards_of):
        draws = jax.random.uniform(jax.random.fold_in(jax.random.fold_in(rng, 6), position), (shards_of,), jnp.float32, smallest / len(pieces), top_value / len(pieces))
        return jnp.repeat(jnp.exp(draws), dims[position] // shards_of).reshape((-1,) + (1,) * (len(dims) - position - 1))

    loudness = one(*pieces[0])
    for cut in pieces[1:]:
        loudness = loudness * one(*cut)
    return loudness


def centred(key, shape, spread, limit, pieces=(), held_as=jnp.bfloat16):
    drawn = jax.random.normal(key, shape, jnp.float32) * spread
    if len(pieces) > 0:
        drawn = block_levels(key, shape, pieces, -0.22, 0.18) * drawn
    return jnp.clip(drawn, min=-limit, max=limit).astype(held_as)


def setup_inputs(seed: int = 0) -> dict:
    arg_keys = jax.random.split(jax.random.key(seed), 9)
    activations = centred(arg_keys[0], (TOKENS, D), 1.0, 6.0, ((0, 256),))
    cotangent = centred(arg_keys[1], (TOKENS, D), 1.0, 6.0, ((0, 256),))
    inner_first = centred(arg_keys[2], (N_COL * D, N_ROW * D), 1.0, 6.0, ((0, 32), (1, 8)))
    inner_second = centred(arg_keys[3], (N_ROW * D, N_COL * D), 1.0, 6.0, ((0, 8), (1, 32)))
    outer_first = centred(arg_keys[4], (D, N_ROW * D), 1.0, 6.0, ((0, 32), (1, 8)), jnp.float32)
    momentum_first = centred(arg_keys[5], (D, N_ROW * D), 0.5, 3.0, ((0, 32), (1, 8)), jnp.float32)
    outer_second = centred(arg_keys[6], (D, N_COL * D), 1.0, 6.0, ((0, 8), (1, 32)), jnp.float32)
    momentum_second = centred(arg_keys[7], (D, N_COL * D), 0.5, 3.0, ((0, 8), (1, 32)), jnp.float32)
    return dict(activations=activations, cotangent=cotangent, inner_first=inner_first, inner_second=inner_second, outer_first=outer_first, momentum_first=momentum_first, outer_second=outer_second, momentum_second=momentum_second)


inner_rate = 1.0
outer_rate = 0.7
momentum_coef = 0.9

def path_step(inputs, grads, first_w, second_w):
    unit_scale = 1.0 / jnp.sqrt(jnp.float32(D))
    hidden = jnp.dot(inputs.astype(jnp.float32), first_w.astype(jnp.float32)) * unit_scale
    logistic = jax.nn.sigmoid(hidden)
    second_in = (hidden * logistic).astype(jnp.bfloat16)
    grad_second = jnp.dot(second_in.astype(jnp.float32).T, grads.astype(jnp.float32)) * unit_scale
    backward = jnp.dot(grads.astype(jnp.float32), second_w.astype(jnp.float32).T) * unit_scale
    first_cot = (backward * logistic * (1.0 + hidden * (1.0 - logistic))).astype(jnp.bfloat16)
    grad_first = jnp.dot(inputs.astype(jnp.float32).T, first_cot.astype(jnp.float32)) * unit_scale
    final_first = first_w.astype(jnp.float32) - inner_rate * grad_first
    final_second = second_w.astype(jnp.float32) - inner_rate * grad_second
    return (final_first, final_second)

def nesterov(outer_flat, moment_flat, summed, count):
    modules = summed.shape[0]
    outer_mods = outer_flat.reshape(D, modules, D).transpose(1, 0, 2)
    moment_mods = moment_flat.reshape(D, modules, D).transpose(1, 0, 2)
    pseudo_grad = outer_mods - summed / count
    moment_new = momentum_coef * moment_mods + pseudo_grad
    outer_new = outer_mods - outer_rate * (pseudo_grad + momentum_coef * moment_new)
    back_outer = outer_new.transpose(1, 0, 2).reshape(D, modules * D)
    back_moment = moment_new.transpose(1, 0, 2).reshape(D, modules * D)
    return (back_outer, back_moment)

def reference(activations, cotangent, inner_first, inner_second, outer_first, momentum_first, outer_second, momentum_second):

    def one_path(path, carry):
        sum_first, sum_second = carry
        path = jnp.asarray(path).astype(jnp.int32)
        grid_row = (path // N_COL).astype(jnp.int32)
        grid_col = (path % N_COL).astype(jnp.int32)
        zero = jnp.asarray(0).astype(jnp.int32)
        inputs = lax.dynamic_slice(activations, ((path * TOK_DEV).astype(jnp.int32), zero), (TOK_DEV, D))
        grads = lax.dynamic_slice(cotangent, ((path * TOK_DEV).astype(jnp.int32), zero), (TOK_DEV, D))
        first_w = lax.dynamic_slice(inner_first, ((grid_col * D).astype(jnp.int32), (grid_row * D).astype(jnp.int32)), (D, D))
        second_w = lax.dynamic_slice(inner_second, ((grid_row * D).astype(jnp.int32), (grid_col * D).astype(jnp.int32)), (D, D))
        final_first, final_second = path_step(inputs, grads, first_w, second_w)
        sum_first = sum_first.at[grid_row].add(final_first)
        sum_second = sum_second.at[grid_col].add(final_second)
        return (sum_first, sum_second)
    start = (jnp.zeros((N_ROW, D, D), jnp.float32), jnp.zeros((N_COL, D, D), jnp.float32))
    sum_first, sum_second = lax.fori_loop(0, N_ROW * N_COL, one_path, start)
    new_outer_first, new_momentum_first = nesterov(outer_first, momentum_first, sum_first, N_COL)
    new_outer_second, new_momentum_second = nesterov(outer_second, momentum_second, sum_second, N_ROW)
    reset_first = jnp.tile(new_outer_first.astype(jnp.bfloat16), (N_COL, 1))
    reset_second = jnp.tile(new_outer_second.astype(jnp.bfloat16), (N_ROW, 1))
    return (new_outer_first, new_momentum_first, new_outer_second, new_momentum_second, reset_first, reset_second)
```

```python
import jax
import jax.numpy as jnp
from jax import lax
from jax.sharding import PartitionSpec as P

inner_rate = 1.0
outer_rate = 0.7
momentum_coef = 0.9

ROWS, COLS = 8, 32
CORE_SWAP = [(i, i ^ 1) for i in range(COLS)]
CHIP_GROUPS = [[2 * k + c for k in range(COLS // 2)] for c in range(2)]


def nesterov(outer_rows, moment_rows, summed, count):
    pseudo_grad = outer_rows - summed / count
    moment_new = momentum_coef * moment_rows + pseudo_grad
    outer_new = outer_rows - outer_rate * (pseudo_grad + momentum_coef * moment_new)
    return (outer_new, moment_new)


def on_device(
    activations,
    cotangent,
    inner_first,
    inner_second,
    outer_first,
    momentum_first,
    outer_second,
    momentum_second,
):
    width = inner_first.shape[0]
    unit_scale = 1.0 / jnp.sqrt(jnp.float32(width))
    rows_second = outer_second.shape[0]
    rows_first = outer_first.shape[0]
    core = lax.axis_index("col") % 2
    hidden = jnp.dot(activations, inner_first, preferred_element_type=jnp.float32) * unit_scale
    logistic = jax.nn.sigmoid(hidden)
    second_in = (hidden * logistic).astype(jnp.bfloat16)
    backward = (
        lax.dot_general(
            cotangent, inner_second, (((1,), (1,)), ((), ())), preferred_element_type=jnp.float32
        )
        * unit_scale
    )
    first_cot = (backward * logistic * (1.0 + hidden * (1.0 - logistic))).astype(jnp.bfloat16)

    def final_rows(inputs, grads, weight):
        grad_rows = (
            lax.dot_general(
                inputs, grads, (((0,), (0,)), ((), ())), preferred_element_type=jnp.float32
            )
            * unit_scale
        )
        return weight.astype(jnp.float32) - inner_rate * grad_rows

    final_first = final_rows(activations, first_cot, inner_first)
    pairs = final_first.reshape(COLS // 2, 2, rows_first, width)
    mine = jnp.where(core == 0, pairs[:, 0], pairs[:, 1])
    theirs = jnp.where(core == 0, pairs[:, 1], pairs[:, 0])
    got = lax.ppermute(theirs, "col", CORE_SWAP)
    chip_first = (mine + got).astype(jnp.bfloat16)

    final_second = final_rows(second_in, cotangent, inner_second).astype(jnp.bfloat16)
    terms_second = lax.all_to_all(
        final_second.reshape(ROWS, rows_second, width), "row", 0, 0
    )
    summed_second = jnp.sum(terms_second.astype(jnp.float32), axis=0)
    new_outer_second, new_momentum_second = nesterov(
        outer_second, momentum_second, summed_second, ROWS
    )

    terms_first = lax.all_to_all(chip_first, "col", 0, 0, axis_index_groups=CHIP_GROUPS)
    summed_first = jnp.sum(terms_first.astype(jnp.float32), axis=0)
    new_outer_first, new_momentum_first = nesterov(
        outer_first, momentum_first, summed_first, COLS
    )

    reset_second = lax.all_to_all(
        jnp.broadcast_to(
            new_outer_second.astype(jnp.bfloat16)[None], (ROWS, rows_second, width)
        ),
        "row",
        0,
        0,
    ).reshape(width, width)
    half = lax.all_to_all(
        jnp.broadcast_to(
            new_outer_first.astype(jnp.bfloat16)[None], (COLS // 2, rows_first, width)
        ),
        "col",
        0,
        0,
        axis_index_groups=CHIP_GROUPS,
    )
    other = lax.ppermute(half, "col", CORE_SWAP)
    even = jnp.where(core == 0, half, other)
    odd = jnp.where(core == 0, other, half)
    reset_first = jnp.stack([even, odd], axis=1).reshape(width, width)
    return (
        new_outer_first,
        new_momentum_first,
        new_outer_second,
        new_momentum_second,
        reset_first,
        reset_second,
    )


def solution(mesh):
    return jax.shard_map(
        on_device,
        mesh=mesh,
        in_specs=(
            P(("row", "col"), None),
            P(("row", "col"), None),
            P("col", "row"),
            P("row", "col"),
            P("col", "row"),
            P("col", "row"),
            P("row", "col"),
            P("row", "col"),
        ),
        out_specs=(
            P("col", "row"),
            P("col", "row"),
            P("row", "col"),
            P("row", "col"),
            P("col", "row"),
            P("row", "col"),
        ),
        check_vma=False,
    )
```

```python
import jax
import jax.numpy as jnp
from jax import lax
from jax.experimental import pallas as pl
from jax.experimental.pallas import tpu as pltpu
from jax.sharding import PartitionSpec as P

F32, BF16 = jnp.float32, jnp.bfloat16
inner_rate = 1.0
outer_rate = 0.7
momentum_coef = 0.9

T, D = 1024, 896
ROWS, COLS = 8, 32
ZL, XS = 2, 4
ZS, YS, CORES = 4, 4, 2
SUB = D // COLS
BLK = ZS * SUB
SUB2 = D // ROWS
TB = 512
RB = 448
X_GROUPS = [[z * XS + x for x in range(XS)] for z in range(ZL)]
UNIT = 1.0 / float(D) ** 0.5
VMEM_BYTES = 32 * 2**20
MOST_VMEM = 60 * 2**20


def shift(dz, dy, dc):
    def index(z, y, c):
        return ((z % ZS) * YS + y % YS) * CORES + c % CORES

    return [
        (index(z, y, c), index(z + dz, y + dy, c + dc))
        for z in range(ZS)
        for y in range(YS)
        for c in range(CORES)
    ]


def dot(a, b, ca, cb):
    return lax.dot_general(a, b, (((ca,), (cb,)), ((), ())), preferred_element_type=F32)


def place():
    col, row = lax.axis_index("col"), lax.axis_index("row")
    y = lax.rem(col // CORES, YS)
    return (col // (YS * CORES), y, lax.rem(col, CORES), row // XS)


def pick(position, options):
    value = options[0]
    for i in range(1, len(options)):
        value = jnp.where(position == i, options[i], value)
    return value


def nesterov(outer_rows, moment_rows, summed, count):
    pseudo_grad = outer_rows - summed / count
    moment_new = momentum_coef * moment_rows + pseudo_grad
    outer_new = outer_rows - outer_rate * (pseudo_grad + momentum_coef * moment_new)
    return (outer_new, moment_new)


def terms_kernel(x_hbm, w1_hbm, g_hbm, w2_hbm, mine, theirs, second, x, w1, g, w2, s, fc, acc, sems):
    def fetch(src, dst, i):
        return pltpu.make_async_copy(src, dst, sems.at[i])

    steps = T // TB
    parts = [pl.ds(t * TB, TB) for t in range(steps)]
    get_w1, get_w2 = fetch(w1_hbm, w1, 0), fetch(w2_hbm, w2, 1)
    get_x = [fetch(x_hbm.at[p], x.at[p], 2 + t) for t, p in enumerate(parts)]
    get_g = [fetch(g_hbm.at[p], g.at[p], 2 + steps + t) for t, p in enumerate(parts)]
    for copy in [get_x[0], get_w1, get_g[0], get_w2]:
        copy.start()
    for t in range(1, steps):
        get_x[t].start()
        get_g[t].start()
    for t, rows in enumerate(parts):
        if t == 0:
            get_w1.wait()
        get_x[t].wait()
        hidden = dot(x[rows, :], w1[...], 1, 0) * UNIT
        logistic = 0.5 * jnp.tanh(0.5 * hidden) + 0.5
        s[rows, :] = (hidden * logistic).astype(BF16)
        if t == 0:
            get_w2.wait()
        get_g[t].wait()
        backward = dot(g[rows, :], w2[...], 1, 1) * UNIT
        fc[rows, :] = (backward * logistic * (1.0 + hidden * (1.0 - logistic))).astype(BF16)
    for r in range(D // RB):
        cols = pl.ds(r * RB, RB)
        acc[cols, :] = w1[cols, :].astype(F32) - inner_rate * UNIT * dot(x[:, cols], fc[...], 0, 0)
        grad_second = UNIT * dot(s[:, cols], g[...], 0, 0)
        second[cols, :] = (w2[cols, :].astype(F32) - inner_rate * grad_second).astype(BF16)
    core = place()[2]
    for z in range(ZS):
        for y in range(YS):
            first = (z * YS + y) * CORES * SUB
            even = acc[pl.ds(first, SUB), :]
            odd = acc[pl.ds(first + SUB, SUB), :]
            rows = pl.ds(BLK * y + SUB * z, SUB)
            mine[rows, :] = jnp.where(core == 0, even, odd)
            theirs[rows, :] = jnp.where(core == 0, odd, even)


def core_sum_kernel(mine, got, own, *sends):
    y = place()[1]
    for k in range(YS):
        rows = pl.ds(pl.multiple_of(lax.rem(y + k, YS) * BLK, 16), BLK)
        block = mine[rows, :] + got[rows, :]
        if k == 0:
            own[...] = block
        else:
            sends[k - 1][...] = block.astype(BF16)


def y_sum_kernel(own, r1, r2, r3, total, o0, o1, o2, o3):
    z = place()[0]
    total[...] = own[...] + r1[...].astype(F32) + r2[...].astype(F32) + r3[...].astype(F32)
    for k, out in enumerate((o0, o1, o2, o3)):
        piece = pick(lax.rem(z + k, ZS), [total[pl.ds(SUB * j, SUB), :] for j in range(ZS)])
        out[...] = piece.astype(out.dtype)


def update_first_kernel(a, b, c, d, outer, moment, new_outer, new_moment, low):
    summed = a[...] + b[...] + c[...].astype(F32) + d[...]
    outer_new, moment_new = nesterov(outer[...], moment[...], summed, ROWS * YS)
    new_outer[...] = outer_new
    new_moment[...] = moment_new
    low[...] = outer_new.astype(BF16)


def join_z_kernel(p0, p1, p2, p3, out, wide):
    z = place()[0]
    pieces = [p[...].astype(F32) for p in (p0, p1, p2, p3)]
    for j in range(ZS):
        wide[pl.ds(SUB * j, SUB), :] = pick(lax.rem(z - j + ZS, ZS), pieces)
    out[...] = wide[...].astype(BF16)


def join_kernel(p0, p1, p2, p3, q0, q1, q2, q3, second, out, second_out, wide, sems):
    copies = [
        pltpu.make_async_copy(
            second.at[x, z], second_out.at[pl.ds((z * XS + x) * SUB2, SUB2)], sems.at[z * XS + x]
        )
        for z in range(ZL)
        for x in range(XS)
    ]
    for copy in copies:
        copy.start()
    _, y, core, _ = place()
    for j in range(YS):
        k = lax.rem(y - j + YS, YS)
        own = pick(k, [p[...] for p in (p0, p1, p2, p3)]).astype(F32)
        other = pick(k, [q[...] for q in (q0, q1, q2, q3)]).astype(F32)
        for c, block in enumerate((jnp.where(core == 0, own, other), jnp.where(core == 0, other, own))):
            for z in range(ZS):
                wide[pl.ds(((z * YS + j) * CORES + c) * SUB, SUB), :] = block[z * SUB : (z + 1) * SUB]
    out[...] = wide[...].astype(BF16)
    for copy in copies:
        copy.wait()


def update_second_kernel(terms, outer_hbm, moment_hbm, new_outer, new_moment, low, outer, moment, sems):
    copies = [
        pltpu.make_async_copy(outer_hbm, outer, sems.at[0]),
        pltpu.make_async_copy(moment_hbm, moment, sems.at[1]),
    ]
    for copy in copies:
        copy.start()
    summed = terms[0].astype(F32)
    for k in range(1, ROWS):
        summed = summed + terms[k].astype(F32)
    for copy in copies:
        copy.wait()
    outer_new, moment_new = nesterov(outer[...], moment[...], summed, ROWS)
    new_outer[...] = outer_new
    new_moment[...] = moment_new
    low[...] = outer_new.astype(BF16)


def spread_kernel(own, other, out):
    z_lo = place()[3]
    first = jnp.where(z_lo == 0, own[...], other[...])
    second = jnp.where(z_lo == 0, other[...], own[...])
    for x in range(XS):
        out[x, 0] = first
        out[x, 1] = second


def call(kernel, args, outs, scratch=(), flops=0, name=None, hbm_args=None, after=(), vmem=VMEM_BYTES):
    inside = pl.BlockSpec(memory_space=pltpu.VMEM)
    outside = pl.BlockSpec(memory_space=pltpu.HBM)
    shapes = tuple(jax.ShapeDtypeStruct(shape, dtype) for shape, dtype in outs)
    moved = sum(a.size * a.dtype.itemsize for a in args)
    moved += sum(s.size * s.dtype.itemsize for s in shapes)
    first, last = len(args), len(args) + len(after)

    def body(*refs):
        kernel(*refs[:first], *refs[last:])

    return pl.pallas_call(
        body,
        out_shape=shapes,
        in_specs=[outside if h else inside for h in (hbm_args or [False] * len(args))]
        + [pl.BlockSpec(memory_space=pl.ANY) for _ in after],
        out_specs=tuple(inside for _ in shapes),
        scratch_shapes=list(scratch),
        compiler_params=pltpu.CompilerParams(vmem_limit_bytes=vmem),
        cost_estimate=pl.CostEstimate(flops=flops, bytes_accessed=moved, transcendentals=0),
        name=name,
    )(*args, *after)


def on_device(
    activations,
    cotangent,
    inner_first,
    inner_second,
    outer_first,
    momentum_first,
    outer_second,
    momentum_second,
):
    def send(value, dz, dy, dc):
        return lax.ppermute(value, "col", shift(dz, dy, dc))

    mine, theirs, final_second = call(
        terms_kernel,
        (activations, inner_first, cotangent, inner_second),
        (((D // 2, D), F32), ((D // 2, D), F32), ((D, D), BF16)),
        [
            pltpu.VMEM((T, D), BF16),
            pltpu.VMEM((D, D), BF16),
            pltpu.VMEM((T, D), BF16),
            pltpu.VMEM((D, D), BF16),
            pltpu.VMEM((T, D), BF16),
            pltpu.VMEM((T, D), BF16),
            pltpu.VMEM((D, D), F32),
            pltpu.SemaphoreType.DMA((2 + 2 * (T // TB),)),
        ],
        flops=8 * T * D * D,
        name="terms",
        hbm_args=(True,) * 4,
        vmem=MOST_VMEM,
    )
    got = send(theirs, 0, 0, 1)
    terms_second = lax.all_to_all(final_second.reshape(ROWS, SUB2, D), "row", 0, 0)

    own, *sends = call(
        core_sum_kernel,
        (mine, got),
        (((BLK, D), F32),) + (((BLK, D), BF16),) * 3,
        name="core_sum",
    )
    y_terms = [send(s, 0, k + 1, 0) for k, s in enumerate(sends)]
    y_total, own, *sends = call(
        y_sum_kernel,
        (own, *y_terms),
        (((BLK, D), F32),) + tuple(((SUB, D), t) for t in (F32, F32, BF16, F32)),
        name="y_sum",
    )
    z_terms = [send(s, k + 1, 0, 0) for k, s in enumerate(sends)]
    new_outer_first, new_momentum_first, low = call(
        update_first_kernel,
        (own, *z_terms, outer_first, momentum_first),
        (((SUB, D), F32), ((SUB, D), F32), ((SUB, D), BF16)),
        name="update_first",
    )

    new_outer_second, new_momentum_second, low_second = call(
        update_second_kernel,
        (terms_second, outer_second, momentum_second),
        (((SUB2, D), F32), ((SUB2, D), F32), ((SUB2, D), BF16)),
        [pltpu.VMEM((SUB2, D), F32), pltpu.VMEM((SUB2, D), F32), pltpu.SemaphoreType.DMA((2,))],
        name="update_second",
        hbm_args=(False, True, True),
        after=(y_total,),
    )
    other_second = lax.ppermute(low_second, "row", [(i, (i + XS) % ROWS) for i in range(ROWS)])
    (spread,) = call(
        spread_kernel,
        (low_second, other_second),
        (((XS, ZL, SUB2, D), BF16),),
        name="spread",
        after=(low,),
    )
    gathered_second = lax.all_to_all(spread, "row", 0, 0, axis_index_groups=X_GROUPS)

    (block,) = call(
        join_z_kernel,
        [low] + [send(low, k, 0, 0) for k in range(1, ZS)],
        (((BLK, D), BF16),),
        [pltpu.VMEM((BLK, D), F32)],
        name="join_z",
    )
    blocks = [block] + [send(block, 0, k, 0) for k in range(1, YS)]
    others = [send(b, 0, 0, 1) for b in blocks]
    vmem, anywhere = pl.BlockSpec(memory_space=pltpu.VMEM), pl.BlockSpec(memory_space=pl.ANY)
    module = jax.ShapeDtypeStruct((D, D), BF16)
    reset_first, reset_second = pl.pallas_call(
        join_kernel,
        out_shape=(module, module),
        in_specs=[vmem] * 8 + [anywhere],
        out_specs=(vmem, anywhere),
        scratch_shapes=[pltpu.VMEM((D, D), F32), pltpu.SemaphoreType.DMA((ROWS,))],
        compiler_params=pltpu.CompilerParams(vmem_limit_bytes=VMEM_BYTES),
        cost_estimate=pl.CostEstimate(flops=0, bytes_accessed=8 * D * D, transcendentals=0),
        name="join",
    )(*blocks, *others, gathered_second)
    return (
        new_outer_first,
        new_momentum_first,
        new_outer_second,
        new_momentum_second,
        reset_first,
        reset_second,
    )


def solution(mesh):
    return jax.shard_map(
        on_device,
        mesh=mesh,
        in_specs=(
            P(("row", "col"), None),
            P(("row", "col"), None),
            P("col", "row"),
            P("row", "col"),
            P("col", "row"),
            P("col", "row"),
            P("row", "col"),
            P("row", "col"),
        ),
        out_specs=(
            P("col", "row"),
            P("col", "row"),
            P("row", "col"),
            P("row", "col"),
            P("col", "row"),
            P("row", "col"),
        ),
        check_vma=False,
    )
```

```python
import jax
import jax.numpy as jnp
from jax import lax
from jax.experimental import pallas as pl
from jax.experimental.pallas import tpu as pltpu
from jax.sharding import PartitionSpec as P

F32, BF16 = jnp.float32, jnp.bfloat16
inner_rate = 1.0
outer_rate = 0.7
momentum_coef = 0.9

T, D = 1024, 896
ROWS, COLS = 8, 32
ZS, YS, CORES = 4, 4, 2
SUB = D // COLS
BLK = ZS * SUB
SUB2 = D // ROWS
TB = 512
RB = 448
UNIT = 1.0 / float(D) ** 0.5
VMEM_BYTES = 32 * 2**20
MOST_VMEM = 60 * 2**20
SOME, LONG = 15 * 10**9, 6 * 10**10


def shift(dz, dy, dc):
    def index(z, y, c):
        return ((z % ZS) * YS + y % YS) * CORES + c % CORES

    return [
        (index(z, y, c), index(z + dz, y + dy, c + dc))
        for z in range(ZS)
        for y in range(YS)
        for c in range(CORES)
    ]


def dot(a, b, ca, cb):
    return lax.dot_general(a, b, (((ca,), (cb,)), ((), ())), preferred_element_type=F32)


def place():
    col = lax.axis_index("col")
    return (col // (YS * CORES), lax.rem(col // CORES, YS), lax.rem(col, CORES))


def pick(position, options):
    value = options[0]
    for i in range(1, len(options)):
        value = jnp.where(position == i, options[i], value)
    return value


def nesterov(outer_rows, moment_rows, summed, count):
    pseudo_grad = outer_rows - summed / count
    moment_new = momentum_coef * moment_rows + pseudo_grad
    outer_new = outer_rows - outer_rate * (pseudo_grad + momentum_coef * moment_new)
    return (outer_new, moment_new)


def terms_kernel(x_hbm, w1_hbm, g_hbm, w2_hbm, mine, theirs, second, x, w1, g, w2, s, fc, acc, sems):
    def fetch(src, dst, i):
        return pltpu.make_async_copy(src, dst, sems.at[i])

    steps = T // TB
    parts = [pl.ds(t * TB, TB) for t in range(steps)]
    get_w1, get_w2 = fetch(w1_hbm, w1, 0), fetch(w2_hbm, w2, 1)
    get_x = [fetch(x_hbm.at[p], x.at[p], 2 + t) for t, p in enumerate(parts)]
    get_g = [fetch(g_hbm.at[p], g.at[p], 2 + steps + t) for t, p in enumerate(parts)]
    for copy in [get_x[0], get_w1, get_g[0], get_w2]:
        copy.start()
    for t in range(1, steps):
        get_x[t].start()
        get_g[t].start()
    for t, rows in enumerate(parts):
        if t == 0:
            get_w1.wait()
        get_x[t].wait()
        hidden = dot(x[rows, :], w1[...], 1, 0) * UNIT
        logistic = 0.5 * jnp.tanh(0.5 * hidden) + 0.5
        s[rows, :] = (hidden * logistic).astype(BF16)
        if t == 0:
            get_w2.wait()
        get_g[t].wait()
        backward = dot(g[rows, :], w2[...], 1, 1) * UNIT
        fc[rows, :] = (backward * logistic * (1.0 + hidden * (1.0 - logistic))).astype(BF16)
    for r in range(D // RB):
        cols = pl.ds(r * RB, RB)
        acc[cols, :] = w1[cols, :].astype(F32) - inner_rate * UNIT * dot(x[:, cols], fc[...], 0, 0)
        grad_second = UNIT * dot(s[:, cols], g[...], 0, 0)
        second[cols, :] = (w2[cols, :].astype(F32) - inner_rate * grad_second).astype(BF16)
    core = place()[2]
    for z in range(ZS):
        for y in range(YS):
            first = (z * YS + y) * CORES * SUB
            even = acc[pl.ds(first, SUB), :]
            odd = acc[pl.ds(first + SUB, SUB), :]
            rows = pl.ds(BLK * y + SUB * z, SUB)
            mine[rows, :] = jnp.where(core == 0, even, odd)
            theirs[rows, :] = jnp.where(core == 0, odd, even)


def core_sum_kernel(mine, got, own, *sends):
    y = place()[1]
    for k in range(YS):
        rows = pl.ds(pl.multiple_of(lax.rem(y + k, YS) * BLK, 16), BLK)
        block = mine[rows, :] + got[rows, :]
        if k == 0:
            own[...] = block
        else:
            sends[k - 1][...] = block.astype(BF16)


def y_sum_kernel(own, r1, r2, r3, total, o0, o1, o2, o3):
    z = place()[0]
    total[...] = own[...] + r1[...].astype(F32) + r2[...].astype(F32) + r3[...].astype(F32)
    for k, out in enumerate((o0, o1, o2, o3)):
        piece = pick(lax.rem(z + k, ZS), [total[pl.ds(SUB * j, SUB), :] for j in range(ZS)])
        out[...] = piece.astype(out.dtype)


def update_first_kernel(a, b, c, d, outer, moment, new_outer, new_moment, low):
    summed = a[...] + b[...] + c[...].astype(F32) + d[...]
    outer_new, moment_new = nesterov(outer[...], moment[...], summed, ROWS * YS)
    new_outer[...] = outer_new
    new_moment[...] = moment_new
    low[...] = outer_new.astype(BF16)


def join_z_kernel(p0, p1, p2, p3, out, wide):
    z = place()[0]
    pieces = [p[...].astype(F32) for p in (p0, p1, p2, p3)]
    for j in range(ZS):
        wide[pl.ds(SUB * j, SUB), :] = pick(lax.rem(z - j + ZS, ZS), pieces)
    out[...] = wide[...].astype(BF16)


def join_kernel(p0, p1, p2, p3, q0, q1, q2, q3, second, out, second_out, wide, sems):
    copies = [pltpu.make_async_copy(second, second_out, sems.at[0])]
    for copy in copies:
        copy.start()
    _, y, core = place()
    for j in range(YS):
        k = lax.rem(y - j + YS, YS)
        own = pick(k, [p[...] for p in (p0, p1, p2, p3)]).astype(F32)
        other = pick(k, [q[...] for q in (q0, q1, q2, q3)]).astype(F32)
        for c, block in enumerate((jnp.where(core == 0, own, other), jnp.where(core == 0, other, own))):
            for z in range(ZS):
                wide[pl.ds(((z * YS + j) * CORES + c) * SUB, SUB), :] = block[z * SUB : (z + 1) * SUB]
    out[...] = wide[...].astype(BF16)
    for copy in copies:
        copy.wait()


def update_second_kernel(terms, outer, moment, new_outer, new_moment, spread):
    summed = terms[0].astype(F32)
    for k in range(1, ROWS):
        summed = summed + terms[k].astype(F32)
    outer_new, moment_new = nesterov(outer[...], moment[...], summed, ROWS)
    new_outer[...] = outer_new
    new_moment[...] = moment_new
    low = outer_new.astype(BF16)
    for k in range(ROWS):
        spread[k] = low


def call(kernel, args, outs, scratch=(), flops=0, name=None, hbm_args=None, after=(), vmem=VMEM_BYTES):
    inside = pl.BlockSpec(memory_space=pltpu.VMEM)
    outside = pl.BlockSpec(memory_space=pltpu.HBM)
    shapes = tuple(jax.ShapeDtypeStruct(shape, dtype) for shape, dtype in outs)
    moved = sum(a.size * a.dtype.itemsize for a in args)
    moved += sum(s.size * s.dtype.itemsize for s in shapes)
    first, last = len(args), len(args) + len(after)

    def body(*refs):
        kernel(*refs[:first], *refs[last:])

    return pl.pallas_call(
        body,
        out_shape=shapes,
        in_specs=[outside if h else inside for h in (hbm_args or [False] * len(args))]
        + [pl.BlockSpec(memory_space=pl.ANY) for _ in after],
        out_specs=tuple(inside for _ in shapes),
        scratch_shapes=list(scratch),
        compiler_params=pltpu.CompilerParams(vmem_limit_bytes=vmem),
        cost_estimate=pl.CostEstimate(flops=flops, bytes_accessed=moved, transcendentals=0),
        name=name,
    )(*args, *after)


def on_device(
    activations,
    cotangent,
    inner_first,
    inner_second,
    outer_first,
    momentum_first,
    outer_second,
    momentum_second,
):
    def send(value, dz, dy, dc):
        return lax.ppermute(value, "col", shift(dz, dy, dc))

    mine, theirs, final_second = call(
        terms_kernel,
        (activations, inner_first, cotangent, inner_second),
        (((D // 2, D), F32), ((D // 2, D), F32), ((D, D), BF16)),
        [
            pltpu.VMEM((T, D), BF16),
            pltpu.VMEM((D, D), BF16),
            pltpu.VMEM((T, D), BF16),
            pltpu.VMEM((D, D), BF16),
            pltpu.VMEM((T, D), BF16),
            pltpu.VMEM((T, D), BF16),
            pltpu.VMEM((D, D), F32),
            pltpu.SemaphoreType.DMA((2 + 2 * (T // TB),)),
        ],
        flops=8 * T * D * D,
        name="terms",
        hbm_args=(True,) * 4,
        vmem=MOST_VMEM,
    )
    got = send(theirs, 0, 0, 1)
    terms_second = lax.all_to_all(final_second.reshape(ROWS, SUB2, D), "row", 0, 0)

    own, *sends = call(
        core_sum_kernel,
        (mine, got),
        (((BLK, D), F32),) + (((BLK, D), BF16),) * 3,
        name="core_sum",
    )
    y_terms = [send(s, 0, k + 1, 0) for k, s in enumerate(sends)]
    y_total, own, *sends = call(
        y_sum_kernel,
        (own, *y_terms),
        (((BLK, D), F32),) + tuple(((SUB, D), t) for t in (F32, F32, BF16, F32)),
        flops=SOME,
        name="y_sum",
    )
    z_terms = [send(s, k + 1, 0, 0) for k, s in enumerate(sends)]
    new_outer_second, new_momentum_second, spread = call(
        update_second_kernel,
        (terms_second, outer_second, momentum_second),
        (((SUB2, D), F32), ((SUB2, D), F32), ((ROWS, SUB2, D), BF16)),
        name="update_second",
        after=(y_total,),
    )
    new_outer_first, new_momentum_first, low = call(
        update_first_kernel,
        (own, *z_terms, outer_first, momentum_first),
        (((SUB, D), F32), ((SUB, D), F32), ((SUB, D), BF16)),
        name="update_first",
        after=(spread,),
    )

    (block,) = call(
        join_z_kernel,
        [low] + [send(low, k, 0, 0) for k in range(1, ZS)],
        (((BLK, D), BF16),),
        [pltpu.VMEM((BLK, D), F32)],
        flops=LONG,
        name="join_z",
    )
    gathered_second = lax.all_to_all(spread, "row", 0, 0)
    blocks = [block] + [send(block, 0, k, 0) for k in range(1, YS)]
    others = [send(b, 0, 0, 1) for b in blocks]
    vmem, anywhere = pl.BlockSpec(memory_space=pltpu.VMEM), pl.BlockSpec(memory_space=pl.ANY)
    module = jax.ShapeDtypeStruct((D, D), BF16)
    reset_first, reset_second = pl.pallas_call(
        join_kernel,
        out_shape=(module, module),
        in_specs=[vmem] * 8 + [anywhere],
        out_specs=(vmem, anywhere),
        scratch_shapes=[pltpu.VMEM((D, D), F32), pltpu.SemaphoreType.DMA((1,))],
        compiler_params=pltpu.CompilerParams(vmem_limit_bytes=VMEM_BYTES),
        cost_estimate=pl.CostEstimate(flops=0, bytes_accessed=8 * D * D, transcendentals=0),
        name="join",
    )(*blocks, *others, gathered_second.reshape(D, D))
    return (
        new_outer_first,
        new_momentum_first,
        new_outer_second,
        new_momentum_second,
        reset_first,
        reset_second,
    )


def solution(mesh):
    return jax.shard_map(
        on_device,
        mesh=mesh,
        in_specs=(
            P(("row", "col"), None),
            P(("row", "col"), None),
            P("col", "row"),
            P("row", "col"),
            P("col", "row"),
            P("col", "row"),
            P("row", "col"),
            P("row", "col"),
        ),
        out_specs=(
            P("col", "row"),
            P("col", "row"),
            P("row", "col"),
            P("row", "col"),
            P("col", "row"),
            P("row", "col"),
        ),
        check_vma=False,
    )
```

```python
import jax
import jax.numpy as jnp
from jax import lax
from jax.experimental import pallas as pl
from jax.experimental.pallas import tpu as pltpu
from jax.sharding import PartitionSpec as P

F32, BF16 = jnp.float32, jnp.bfloat16
inner_rate = 1.0
outer_rate = 0.7
momentum_coef = 0.9

T, D = 1024, 896
ROWS, COLS = 8, 32
ZS, YS, CORES = 4, 4, 2
SUB = D // COLS
BLK = ZS * SUB
SUB2 = D // ROWS
TB = 512
RB = 448
UNIT = 1.0 / float(D) ** 0.5
VMEM_BYTES = 32 * 2**20
MOST_VMEM = 60 * 2**20
SOME, LONG = 15 * 10**9, 6 * 10**10


def shift(dz, dy, dc):
    def index(z, y, c):
        return ((z % ZS) * YS + y % YS) * CORES + c % CORES

    return [
        (index(z, y, c), index(z + dz, y + dy, c + dc))
        for z in range(ZS)
        for y in range(YS)
        for c in range(CORES)
    ]


def dot(a, b, ca, cb):
    return lax.dot_general(a, b, (((ca,), (cb,)), ((), ())), preferred_element_type=F32)


def place():
    col = lax.axis_index("col")
    return (col // (YS * CORES), lax.rem(col // CORES, YS), lax.rem(col, CORES))


def pick(position, options):
    value = options[0]
    for i in range(1, len(options)):
        value = jnp.where(position == i, options[i], value)
    return value


def nesterov(outer_rows, moment_rows, summed, count):
    pseudo_grad = outer_rows - summed / count
    moment_new = momentum_coef * moment_rows + pseudo_grad
    outer_new = outer_rows - outer_rate * (pseudo_grad + momentum_coef * moment_new)
    return (outer_new, moment_new)


def terms_kernel(
    x_hbm, w1_hbm, g_hbm, w2_hbm, mine, theirs, second_hbm, x, w1, g, w2, s, fc, acc, halves, second, sems
):
    def fetch(src, dst, i):
        return pltpu.make_async_copy(src, dst, sems.at[i])

    steps = T // TB
    parts = [pl.ds(t * TB, TB) for t in range(steps)]
    get_w1, get_w2 = fetch(w1_hbm, w1, 0), fetch(w2_hbm, w2, 1)
    get_x = [fetch(x_hbm.at[p], x.at[p], 2 + t) for t, p in enumerate(parts)]
    get_g = [fetch(g_hbm.at[p], g.at[p], 2 + steps + t) for t, p in enumerate(parts)]
    for copy in [get_x[0], get_w1, get_g[0], get_w2]:
        copy.start()
    for t in range(1, steps):
        get_x[t].start()
        get_g[t].start()
    for t, rows in enumerate(parts):
        if t == 0:
            get_w1.wait()
        get_x[t].wait()
        hidden = dot(x[rows, :], w1[...], 1, 0) * UNIT
        logistic = 0.5 * jnp.tanh(0.5 * hidden) + 0.5
        s[rows, :] = (hidden * logistic).astype(BF16)
        if t == 0:
            get_w2.wait()
        get_g[t].wait()
        backward = dot(g[rows, :], w2[...], 1, 1) * UNIT
        fc[rows, :] = (backward * logistic * (1.0 + hidden * (1.0 - logistic))).astype(BF16)
    tiles = [pl.ds(r * RB, RB) for r in range(D // RB)]
    for cols in tiles:
        acc[cols, :] = w1[cols, :].astype(F32) - inner_rate * UNIT * dot(x[:, cols], fc[...], 0, 0)
    core = place()[2]
    for z in range(ZS):
        for y in range(YS):
            first = (z * YS + y) * CORES * SUB
            rows = pl.ds(BLK * y + SUB * z, SUB)
            halves[core, rows, :] = acc[pl.ds(first, SUB), :]
            halves[1 - core, rows, :] = acc[pl.ds(first + SUB, SUB), :]
    puts = [fetch(halves.at[1], theirs, 0), fetch(halves.at[0], mine, 1)]
    for copy in puts:
        copy.start()
    for r, cols in enumerate(tiles):
        grad_second = UNIT * dot(s[:, cols], g[...], 0, 0)
        second[cols, :] = (w2[cols, :].astype(F32) - inner_rate * grad_second).astype(BF16)
        puts.append(fetch(second.at[cols], second_hbm.at[cols], 2 + r))
        puts[-1].start()
    for copy in puts:
        copy.wait()


def core_sum_kernel(mine, got, own, *sends):
    y = place()[1]
    for k in range(YS):
        rows = pl.ds(pl.multiple_of(lax.rem(y + k, YS) * BLK, 16), BLK)
        block = mine[rows, :] + got[rows, :]
        if k == 0:
            own[...] = block
        else:
            sends[k - 1][...] = block.astype(BF16)


def y_sum_kernel(own, r1, r2, r3, o0, o1, o2, o3, total):
    z = place()[0]
    total[...] = own[...] + r1[...].astype(F32) + r2[...].astype(F32) + r3[...].astype(F32)
    for k, out in enumerate((o0, o1, o2, o3)):
        piece = pick(lax.rem(z + k, ZS), [total[pl.ds(SUB * j, SUB), :] for j in range(ZS)])
        out[...] = piece.astype(out.dtype)


def update_first_kernel(a, b, c, d, outer, moment, new_outer, new_moment, low):
    summed = a[...] + b[...] + c[...].astype(F32) + d[...]
    outer_new, moment_new = nesterov(outer[...], moment[...], summed, ROWS * YS)
    new_outer[...] = outer_new
    new_moment[...] = moment_new
    low[...] = outer_new.astype(BF16)


def join_z_kernel(p0, p1, p2, p3, out, wide):
    z = place()[0]
    pieces = [p[...].astype(F32) for p in (p0, p1, p2, p3)]
    for j in range(ZS):
        wide[pl.ds(SUB * j, SUB), :] = pick(lax.rem(z - j + ZS, ZS), pieces)
    out[...] = wide[...].astype(BF16)


def join_kernel(p0, p1, p2, p3, q0, q1, q2, q3, out, wide, low, sems):
    _, y, core = place()
    sides = []
    for j in range(YS):
        k = lax.rem(y - j + YS, YS)
        own = pick(k, [p[...] for p in (p0, p1, p2, p3)]).astype(F32)
        other = pick(k, [q[...] for q in (q0, q1, q2, q3)]).astype(F32)
        sides.append((jnp.where(core == 0, own, other), jnp.where(core == 0, other, own)))
    copies = []
    for z in range(ZS):
        for j in range(YS):
            for c in range(CORES):
                rows = pl.ds(((z * YS + j) * CORES + c) * SUB, SUB)
                wide[rows, :] = sides[j][c][z * SUB : (z + 1) * SUB]
        part = pl.ds(z * YS * CORES * SUB, YS * CORES * SUB)
        low[part, :] = wide[part, :].astype(BF16)
        copies.append(pltpu.make_async_copy(low.at[part], out.at[part], sems.at[z]))
        copies[-1].start()
    for copy in copies:
        copy.wait()


def update_second_kernel(terms, outer, moment, new_outer, new_moment, spread):
    summed = terms[0].astype(F32)
    for k in range(1, ROWS):
        summed = summed + terms[k].astype(F32)
    outer_new, moment_new = nesterov(outer[...], moment[...], summed, ROWS)
    new_outer[...] = outer_new
    new_moment[...] = moment_new
    low = outer_new.astype(BF16)
    for k in range(ROWS):
        spread[k] = low


def call(kernel, args, outs, scratch=(), flops=0, name=None, hbm_args=None, after=(), vmem=VMEM_BYTES, hbm_outs=False):
    inside = pl.BlockSpec(memory_space=pltpu.VMEM)
    outside = pl.BlockSpec(memory_space=pltpu.HBM)
    shapes = tuple(jax.ShapeDtypeStruct(shape, dtype) for shape, dtype in outs)
    moved = sum(a.size * a.dtype.itemsize for a in args)
    moved += sum(s.size * s.dtype.itemsize for s in shapes)
    first, last = len(args), len(args) + len(after)

    def body(*refs):
        kernel(*refs[:first], *refs[last:])

    return pl.pallas_call(
        body,
        out_shape=shapes,
        in_specs=[outside if h else inside for h in (hbm_args or [False] * len(args))]
        + [pl.BlockSpec(memory_space=pl.ANY) for _ in after],
        out_specs=tuple(outside if hbm_outs else inside for _ in shapes),
        scratch_shapes=list(scratch),
        compiler_params=pltpu.CompilerParams(vmem_limit_bytes=vmem),
        cost_estimate=pl.CostEstimate(flops=flops, bytes_accessed=moved, transcendentals=0),
        name=name,
    )(*args, *after)


def on_device(
    activations,
    cotangent,
    inner_first,
    inner_second,
    outer_first,
    momentum_first,
    outer_second,
    momentum_second,
):
    def send(value, dz, dy, dc):
        return lax.ppermute(value, "col", shift(dz, dy, dc))

    mine, theirs, final_second = call(
        terms_kernel,
        (activations, inner_first, cotangent, inner_second),
        (((D // 2, D), F32), ((D // 2, D), F32), ((D, D), BF16)),
        [
            pltpu.VMEM((T, D), BF16),
            pltpu.VMEM((D, D), BF16),
            pltpu.VMEM((T, D), BF16),
            pltpu.VMEM((D, D), BF16),
            pltpu.VMEM((T, D), BF16),
            pltpu.VMEM((T, D), BF16),
            pltpu.VMEM((D, D), F32),
            pltpu.VMEM((CORES, D // 2, D), F32),
            pltpu.VMEM((D, D), BF16),
            pltpu.SemaphoreType.DMA((2 + 2 * (T // TB),)),
        ],
        flops=8 * T * D * D,
        hbm_outs=True,
        name="terms",
        hbm_args=(True,) * 4,
        vmem=MOST_VMEM,
    )
    got = send(theirs, 0, 0, 1)
    terms_second = lax.all_to_all(final_second.reshape(ROWS, SUB2, D), "row", 0, 0)

    own, *sends = call(
        core_sum_kernel,
        (mine, got),
        (((BLK, D), F32),) + (((BLK, D), BF16),) * 3,
        name="core_sum",
    )
    y_terms = [send(s, 0, k + 1, 0) for k, s in enumerate(sends)]
    own, *sends = call(
        y_sum_kernel,
        (own, *y_terms),
        tuple(((SUB, D), t) for t in (F32, F32, BF16, F32)),
        [pltpu.VMEM((BLK, D), F32)],
        flops=SOME,
        name="y_sum",
    )
    z_terms = [send(s, k + 1, 0, 0) for k, s in enumerate(sends)]
    new_outer_second, new_momentum_second, spread = call(
        update_second_kernel,
        (terms_second, outer_second, momentum_second),
        (((SUB2, D), F32), ((SUB2, D), F32), ((ROWS, SUB2, D), BF16)),
        name="update_second",
        after=(own,),
    )
    new_outer_first, new_momentum_first, low = call(
        update_first_kernel,
        (own, *z_terms, outer_first, momentum_first),
        (((SUB, D), F32), ((SUB, D), F32), ((SUB, D), BF16)),
        name="update_first",
        after=(spread,),
    )

    (block,) = call(
        join_z_kernel,
        [low] + [send(low, k, 0, 0) for k in range(1, ZS)],
        (((BLK, D), BF16),),
        [pltpu.VMEM((BLK, D), F32)],
        flops=LONG,
        name="join_z",
    )
    reset_second = lax.all_to_all(spread, "row", 0, 0).reshape(D, D)
    blocks = [block] + [send(block, 0, k, 0) for k in range(1, YS)]
    others = [send(b, 0, 0, 1) for b in blocks]
    (reset_first,) = call(
        join_kernel,
        (*blocks, *others),
        (((D, D), BF16),),
        [pltpu.VMEM((D, D), F32), pltpu.VMEM((D, D), BF16), pltpu.SemaphoreType.DMA((ZS,))],
        name="join",
        hbm_outs=True,
    )
    return (
        new_outer_first,
        new_momentum_first,
        new_outer_second,
        new_momentum_second,
        reset_first,
        reset_second,
    )


def solution(mesh):
    return jax.shard_map(
        on_device,
        mesh=mesh,
        in_specs=(
            P(("row", "col"), None),
            P(("row", "col"), None),
            P("col", "row"),
            P("row", "col"),
            P("col", "row"),
            P("col", "row"),
            P("row", "col"),
            P("row", "col"),
        ),
        out_specs=(
            P("col", "row"),
            P("col", "row"),
            P("row", "col"),
            P("row", "col"),
            P("col", "row"),
            P("row", "col"),
        ),
        check_vma=False,
    )
```

```python
import jax
import jax.numpy as jnp
from jax import lax
from jax.experimental import pallas as pl
from jax.experimental.pallas import tpu as pltpu
from jax.sharding import PartitionSpec as P

F32, BF16 = jnp.float32, jnp.bfloat16
inner_rate = 1.0
outer_rate = 0.7
momentum_coef = 0.9

T, D = 1024, 896
ROWS, COLS = 8, 32
ZS, YS, CORES = 4, 4, 2
SUB = D // COLS
BLK = ZS * SUB
SUB2 = D // ROWS
TB = 512
RB = 224
UNIT = 1.0 / float(D) ** 0.5
VMEM_BYTES = 32 * 2**20
MOST_VMEM = 60 * 2**20
SOME, LONG = 15 * 10**9, 6 * 10**10


def shift(dz, dy, dc):
    def index(z, y, c):
        return ((z % ZS) * YS + y % YS) * CORES + c % CORES

    return [
        (index(z, y, c), index(z + dz, y + dy, c + dc))
        for z in range(ZS)
        for y in range(YS)
        for c in range(CORES)
    ]


def dot(a, b, ca, cb):
    return lax.dot_general(a, b, (((ca,), (cb,)), ((), ())), preferred_element_type=F32)


def place():
    col = lax.axis_index("col")
    return (col // (YS * CORES), lax.rem(col // CORES, YS), lax.rem(col, CORES))


def pick(position, options):
    value = options[0]
    for i in range(1, len(options)):
        value = jnp.where(position == i, options[i], value)
    return value


def nesterov(outer_rows, moment_rows, summed, count):
    pseudo_grad = outer_rows - summed / count
    moment_new = momentum_coef * moment_rows + pseudo_grad
    outer_new = outer_rows - outer_rate * (pseudo_grad + momentum_coef * moment_new)
    return (outer_new, moment_new)


def terms_kernel(
    x_hbm, w1_hbm, g_hbm, w2_hbm, mine, theirs, second_hbm, x, w1, g, w2, s, fc, acc, halves, second, sems
):
    def fetch(src, dst, i):
        return pltpu.make_async_copy(src, dst, sems.at[i])

    steps = T // TB
    parts = [pl.ds(t * TB, TB) for t in range(steps)]
    get_w1, get_w2 = fetch(w1_hbm, w1, 0), fetch(w2_hbm, w2, 1)
    get_x = [fetch(x_hbm.at[p], x.at[p], 2 + t) for t, p in enumerate(parts)]
    get_g = [fetch(g_hbm.at[p], g.at[p], 2 + steps + t) for t, p in enumerate(parts)]
    for copy in [get_x[0], get_w1, get_g[0], get_w2]:
        copy.start()
    for t in range(1, steps):
        get_x[t].start()
        get_g[t].start()
    for t, rows in enumerate(parts):
        if t == 0:
            get_w1.wait()
        get_x[t].wait()
        hidden = dot(x[rows, :], w1[...], 1, 0) * UNIT
        logistic = 0.5 * jnp.tanh(0.5 * hidden) + 0.5
        s[rows, :] = (hidden * logistic).astype(BF16)
        if t == 0:
            get_w2.wait()
        get_g[t].wait()
        backward = dot(g[rows, :], w2[...], 1, 1) * UNIT
        fc[rows, :] = (backward * logistic * (1.0 + hidden * (1.0 - logistic))).astype(BF16)
    tiles = [pl.ds(r * RB, RB) for r in range(D // RB)]
    for cols in tiles:
        acc[cols, :] = w1[cols, :].astype(F32) - inner_rate * UNIT * dot(x[:, cols], fc[...], 0, 0)
    core = place()[2]
    for z in range(ZS):
        for y in range(YS):
            first = (z * YS + y) * CORES * SUB
            rows = pl.ds(BLK * y + SUB * z, SUB)
            halves[core, rows, :] = acc[pl.ds(first, SUB), :]
            halves[1 - core, rows, :] = acc[pl.ds(first + SUB, SUB), :]
    puts = [fetch(halves.at[1], theirs, 0), fetch(halves.at[0], mine, 1)]
    for copy in puts:
        copy.start()
    for r, cols in enumerate(tiles):
        grad_second = UNIT * dot(s[:, cols], g[...], 0, 0)
        second[cols, :] = (w2[cols, :].astype(F32) - inner_rate * grad_second).astype(BF16)
        puts.append(fetch(second.at[cols], second_hbm.at[cols], 2 + r))
        puts[-1].start()
    for copy in puts:
        copy.wait()


def core_sum_kernel(mine, got, own, *sends):
    y = place()[1]
    for k in range(YS):
        rows = pl.ds(pl.multiple_of(lax.rem(y + k, YS) * BLK, 16), BLK)
        block = mine[rows, :] + got[rows, :]
        if k == 0:
            own[...] = block
        else:
            sends[k - 1][...] = block.astype(BF16)


def y_sum_kernel(own, r1, r2, r3, o0, o1, o2, o3, total):
    z = place()[0]
    total[...] = own[...] + r1[...].astype(F32) + r2[...].astype(F32) + r3[...].astype(F32)
    for k, out in enumerate((o0, o1, o2, o3)):
        piece = pick(lax.rem(z + k, ZS), [total[pl.ds(SUB * j, SUB), :] for j in range(ZS)])
        out[...] = piece.astype(out.dtype)


def update_first_kernel(a, b, c, d, outer, moment, new_outer, new_moment, low):
    summed = a[...] + b[...] + c[...].astype(F32) + d[...]
    outer_new, moment_new = nesterov(outer[...], moment[...], summed, ROWS * YS)
    new_outer[...] = outer_new
    new_moment[...] = moment_new
    low[...] = outer_new.astype(BF16)


def join_z_kernel(p0, p1, p2, p3, out, wide):
    z = place()[0]
    pieces = [p[...].astype(F32) for p in (p0, p1, p2, p3)]
    for j in range(ZS):
        wide[pl.ds(SUB * j, SUB), :] = pick(lax.rem(z - j + ZS, ZS), pieces)
    out[...] = wide[...].astype(BF16)


def join_kernel(p0, p1, p2, p3, q0, q1, q2, q3, out, wide, low, sems):
    _, y, core = place()
    sides = []
    for j in range(YS):
        k = lax.rem(y - j + YS, YS)
        own = pick(k, [p[...] for p in (p0, p1, p2, p3)]).astype(F32)
        other = pick(k, [q[...] for q in (q0, q1, q2, q3)]).astype(F32)
        sides.append((jnp.where(core == 0, own, other), jnp.where(core == 0, other, own)))
    copies = []
    for z in range(ZS):
        for j in range(YS):
            for c in range(CORES):
                rows = pl.ds(((z * YS + j) * CORES + c) * SUB, SUB)
                wide[rows, :] = sides[j][c][z * SUB : (z + 1) * SUB]
        part = pl.ds(z * YS * CORES * SUB, YS * CORES * SUB)
        low[part, :] = wide[part, :].astype(BF16)
        copies.append(pltpu.make_async_copy(low.at[part], out.at[part], sems.at[z]))
        copies[-1].start()
    for copy in copies:
        copy.wait()


def update_second_kernel(terms, outer, moment, new_outer, new_moment, spread):
    summed = terms[0].astype(F32)
    for k in range(1, ROWS):
        summed = summed + terms[k].astype(F32)
    outer_new, moment_new = nesterov(outer[...], moment[...], summed, ROWS)
    new_outer[...] = outer_new
    new_moment[...] = moment_new
    low = outer_new.astype(BF16)
    for k in range(ROWS):
        spread[k] = low


def call(kernel, args, outs, scratch=(), flops=0, name=None, hbm_args=None, after=(), vmem=VMEM_BYTES, hbm_outs=False):
    inside = pl.BlockSpec(memory_space=pltpu.VMEM)
    outside = pl.BlockSpec(memory_space=pltpu.HBM)
    shapes = tuple(jax.ShapeDtypeStruct(shape, dtype) for shape, dtype in outs)
    moved = sum(a.size * a.dtype.itemsize for a in args)
    moved += sum(s.size * s.dtype.itemsize for s in shapes)
    first, last = len(args), len(args) + len(after)

    def body(*refs):
        kernel(*refs[:first], *refs[last:])

    return pl.pallas_call(
        body,
        out_shape=shapes,
        in_specs=[outside if h else inside for h in (hbm_args or [False] * len(args))]
        + [pl.BlockSpec(memory_space=pl.ANY) for _ in after],
        out_specs=tuple(outside if hbm_outs else inside for _ in shapes),
        scratch_shapes=list(scratch),
        compiler_params=pltpu.CompilerParams(vmem_limit_bytes=vmem),
        cost_estimate=pl.CostEstimate(flops=flops, bytes_accessed=moved, transcendentals=0),
        name=name,
    )(*args, *after)


def on_device(
    activations,
    cotangent,
    inner_first,
    inner_second,
    outer_first,
    momentum_first,
    outer_second,
    momentum_second,
):
    def send(value, dz, dy, dc):
        return lax.ppermute(value, "col", shift(dz, dy, dc))

    mine, theirs, final_second = call(
        terms_kernel,
        (activations, inner_first, cotangent, inner_second),
        (((D // 2, D), F32), ((D // 2, D), F32), ((D, D), BF16)),
        [
            pltpu.VMEM((T, D), BF16),
            pltpu.VMEM((D, D), BF16),
            pltpu.VMEM((T, D), BF16),
            pltpu.VMEM((D, D), BF16),
            pltpu.VMEM((T, D), BF16),
            pltpu.VMEM((T, D), BF16),
            pltpu.VMEM((D, D), F32),
            pltpu.VMEM((CORES, D // 2, D), F32),
            pltpu.VMEM((D, D), BF16),
            pltpu.SemaphoreType.DMA((2 + 2 * (T // TB),)),
        ],
        flops=8 * T * D * D,
        hbm_outs=True,
        name="terms",
        hbm_args=(True,) * 4,
        vmem=MOST_VMEM,
    )
    got = send(theirs, 0, 0, 1)
    terms_second = lax.all_to_all(final_second.reshape(ROWS, SUB2, D), "row", 0, 0)

    own, *sends = call(
        core_sum_kernel,
        (mine, got),
        (((BLK, D), F32),) + (((BLK, D), BF16),) * 3,
        name="core_sum",
    )
    far = send(sends[1], 0, 2, 0)
    y_terms = [send(sends[0], 0, 1, 0), far, send(sends[2], 0, 3, 0)]
    own, *sends = call(
        y_sum_kernel,
        (own, y_terms[1], y_terms[0], y_terms[2]),
        tuple(((SUB, D), t) for t in (F32, F32, BF16, F32)),
        [pltpu.VMEM((BLK, D), F32)],
        flops=SOME,
        name="y_sum",
    )
    z_terms = [send(s, k + 1, 0, 0) for k, s in enumerate(sends)]
    new_outer_second, new_momentum_second, spread = call(
        update_second_kernel,
        (terms_second, outer_second, momentum_second),
        (((SUB2, D), F32), ((SUB2, D), F32), ((ROWS, SUB2, D), BF16)),
        name="update_second",
        after=(own,),
    )
    new_outer_first, new_momentum_first, low = call(
        update_first_kernel,
        (own, *z_terms, outer_first, momentum_first),
        (((SUB, D), F32), ((SUB, D), F32), ((SUB, D), BF16)),
        name="update_first",
        after=(spread,),
    )

    (block,) = call(
        join_z_kernel,
        [low] + [send(low, k, 0, 0) for k in range(1, ZS)],
        (((BLK, D), BF16),),
        [pltpu.VMEM((BLK, D), F32)],
        flops=LONG,
        name="join_z",
    )
    reset_second = lax.all_to_all(spread, "row", 0, 0).reshape(D, D)
    blocks = [block] + [send(block, 0, k, 0) for k in range(1, YS)]
    others = [send(b, 0, 0, 1) for b in blocks]
    (reset_first,) = call(
        join_kernel,
        (*blocks, *others),
        (((D, D), BF16),),
        [pltpu.VMEM((D, D), F32), pltpu.VMEM((D, D), BF16), pltpu.SemaphoreType.DMA((ZS,))],
        name="join",
        hbm_outs=True,
    )
    return (
        new_outer_first,
        new_momentum_first,
        new_outer_second,
        new_momentum_second,
        reset_first,
        reset_second,
    )


def solution(mesh):
    return jax.shard_map(
        on_device,
        mesh=mesh,
        in_specs=(
            P(("row", "col"), None),
            P(("row", "col"), None),
            P("col", "row"),
            P("row", "col"),
            P("col", "row"),
            P("col", "row"),
            P("row", "col"),
            P("row", "col"),
        ),
        out_specs=(
            P("col", "row"),
            P("col", "row"),
            P("row", "col"),
            P("row", "col"),
            P("col", "row"),
            P("row", "col"),
        ),
        check_vma=False,
    )
```
